32 devices in a mesh: groups: 2 (over y), tp: 4 (over z), sp: 2 (over x), ep: 2 (over core).
Axes of the slice: x: 2, y: 2, z: 4, core: 2. Of those that a mesh axis runs over, the one named last changes fastest.
Arguments:
- activations: bfloat16 [4096, 8192], P(('groups', 'sp'), 'tp'), parts along dimension 0, may hold values from -6 to 6
- output_projection_weight: bfloat16 [8192, 8192], P('tp'), may hold values from -0.09375 to 0.09375
- shrink_matrices: bfloat16 [32, 8192, 64], P(('sp', 'ep'), 'tp'), may hold values from -0.0625 to 0.0625
- expand_matrices: bfloat16 [32, 64, 8192], P(('sp', 'ep'), None, 'tp'), may hold values from -0.75 to 0.75
- tenant_of_block: int32 [32], P(('groups', 'sp')), parts along dimension 0, may hold values from 0 to 31
- token_rows_per_block: int32 [32], P(('groups', 'sp')), parts along dimension 0, may hold values from 1 to 128, as said below
- tenant_table_row: int32 [32], replicated, may hold values from 0 to 31, each once
Outputs:
- projected: bfloat16 [4096, 8192], P(('groups', 'sp'), 'tp'), parts along dimension 0
The draws below stay inside these ranges and needn't reach their ends.
There are 2 independent parts, one for each index of `groups`. The reference program is written for one: setup_inputs(seed, part) draws one part's arguments, and reference() takes and returns one part's arrays. A program takes and returns all parts, laid end to end along the dimension named above; an argument that names none is the same for every part. Nothing has to cross between parts.
Inputs may be any that keep to these rules, and one draw needn't show every extreme that they name: `token_rows_per_block`: each index of sp holds at least one block with all 128 rows live. `tenant_table_row`: each tenant id appears once.
All inputs are finite; a program needn't handle non-finite values.
Results may differ from the reference program's by a relative error of at most 0.012.
Values may be sent and summed in bfloat16 or wider, within the bound.
A program may use at most 192 MiB of HBM per device.

```python
import math
import jax
import jax.numpy as jnp
import numpy as np
from jax import lax

MODEL_WIDTH = 8192
ADAPTER_RANK = 64
BLOCK = 128
BLK_DEV = 8
ADAPTER_COUNT = 32
BLOCKS = 16
TOKENS = 2048
N_TP = 4


def draw_token_rows_per_block(key, part):
    key = jax.random.fold_in(key, 11)
    first_key, second_key = jax.random.split(key)
    random_rows = jax.random.randint(first_key, (BLOCKS,), 1, BLOCK + 1)
    owners = BLOCKS // BLK_DEV
    full_position = jax.random.randint(second_key, (owners,), 0, BLK_DEV)
    block_index = jnp.arange(BLOCKS)
    is_full = block_index % BLK_DEV == full_position[block_index // BLK_DEV]
    return jnp.where(is_full, BLOCK, random_rows).astype(jnp.int32)


def with_ends(drawn, stream_key, least, largest):
    longest = drawn.shape.index(max(drawn.shape))
    spots = []
    for shift in (0, 1):
        where = [jax.random.randint(jax.random.fold_in(stream_key, axis), (), 0, length) for axis, length in enumerate(drawn.shape)]
        where[longest] = (where[longest] + shift) % drawn.shape[longest]
        spots.append(tuple(where))
    return drawn.at[spots[0]].set(least).at[spots[1]].set(largest)


def raised(values, stream_key, source, target, shards_of, factor):
    def block_of(axis_at):
        return (jnp.arange(values.shape[axis_at]) // (values.shape[axis_at] // shards_of)).reshape((-1,) + (1,) * (values.ndim - 1 - axis_at))

    one_side = jax.random.permutation(stream_key, shards_of)[block_of(target)]
    far = (block_of(target) + shards_of // 2) % shards_of
    return jnp.where((block_of(source) == one_side) | (block_of(source) == far), factor * values, values)


def level_of(own_key, extent, cuts, smallest, top_value):
    level = 1.0
    for axis_at, blocks in cuts:
        heights = jax.random.uniform(jax.random.fold_in(jax.random.fold_in(own_key, 6), axis_at), (blocks,), jnp.float32, smallest / len(cuts), top_value / len(cuts))
        level = level * jnp.repeat(jnp.exp(heights), extent[axis_at] // blocks).reshape((-1,) + (1,) * (len(extent) - 1 - axis_at))
    return level


def rank_bounds(number_of, slope):
    portions = [(1 << 20) // math.isqrt(rank ** slope) + 1 for rank in range(1, number_of + 1)]
    spread = 1 + sum(portions) // (1 << 30)
    return np.cumsum(np.array([max(1, weight // spread) for weight in portions]))


def ranked(key, dims, count, slope):
    table = rank_bounds(count, slope)
    pick = jax.random.randint(jax.random.fold_in(key, 1), dims, 0, int(table[count - 1]))
    grade = jnp.searchsorted(jnp.asarray(table, jnp.int32), pick, side="right")
    return jax.random.permutation(jax.random.fold_in(key, 2), count)[grade].astype(jnp.int32)


def normal_values(key, extent, scale, limit, pieces=(), kind=jnp.bfloat16):
    loudness = level_of(key, extent, pieces, -0.22, 0.18) if pieces else 1.0
    array = jax.random.normal(key, extent, jnp.float32) * scale * loudness
    return jnp.minimum(jnp.maximum(array, -limit), limit).astype(kind)


def gaussian_with(own_key, dims, deviation, reach, cuts, heavy, kind=jnp.bfloat16):
    array = deviation * jax.random.normal(own_key, dims, jnp.float32)
    if cuts:
        array = array * level_of(own_key, dims, cuts, -0.22, 0.18)
    return jnp.clip(raised(array, jax.random.fold_in(own_key, 3), *heavy), -reach, reach).astype(kind)


def setup_inputs(seed: int = 0, part: int = 0) -> dict:
    arg_keys = jax.random.split(jax.random.key(seed), 8)
    own_keys = jax.random.split(jax.random.fold_in(arg_keys[7], part), 8)
    activations = normal_values(own_keys[0], (TOKENS, MODEL_WIDTH), 1.0, 6.0, ((0, 2), (1, 4)))
    output_projection_weight = gaussian_with(arg_keys[1], (MODEL_WIDTH, MODEL_WIDTH), MODEL_WIDTH ** -0.5, 0.09375, ((0, 4),), (0, 1, 4, 2.0))
    shrink_matrices = normal_values(arg_keys[2], (ADAPTER_COUNT, MODEL_WIDTH, ADAPTER_RANK), MODEL_WIDTH ** -0.5, 0.0625, ((0, 4), (1, 4)))
    expand_matrices = normal_values(arg_keys[3], (ADAPTER_COUNT, ADAPTER_RANK, MODEL_WIDTH), ADAPTER_RANK ** -0.5, 0.75, ((0, 4), (2, 4)))
    tenant_of_block = with_ends(ranked(own_keys[4], (BLOCKS,), ADAPTER_COUNT, 2), jax.random.fold_in(own_keys[4], 3), 0, ADAPTER_COUNT - 1).astype(jnp.int32)
    token_rows_per_block = draw_token_rows_per_block(jax.random.fold_in(jax.random.fold_in(arg_keys[7], part), 71), part)
    tenant_table_row = jax.random.permutation(arg_keys[6], ADAPTER_COUNT).astype(jnp.int32)
    return {"activations": activations, "output_projection_weight": output_projection_weight, "shrink_matrices": shrink_matrices, "expand_matrices": expand_matrices, "tenant_of_block": tenant_of_block, "token_rows_per_block": token_rows_per_block, "tenant_table_row": tenant_table_row}


def reference(activations, output_projection_weight, shrink_matrices, expand_matrices, tenant_of_block, token_rows_per_block, tenant_table_row):
    tokens = activations.shape[0]
    shard_width = MODEL_WIDTH // N_TP
    block_table_rows = tenant_table_row[tenant_of_block].astype(jnp.int32)
    parts_x = activations.reshape(tokens, N_TP, shard_width).transpose(1, 0, 2)
    parts_w = output_projection_weight.reshape(N_TP, shard_width, MODEL_WIDTH)

    def shard_term(carry, pair):
        x_part, w_part = pair
        term = jnp.dot(x_part, w_part, preferred_element_type=jnp.float32).astype(jnp.bfloat16)
        term = lax.optimization_barrier(term)
        return carry + term.astype(jnp.float32), None

    base, _ = lax.scan(shard_term, jnp.zeros((tokens, MODEL_WIDTH), jnp.float32), (parts_x, parts_w))
    blocked = activations.reshape(-1, BLOCK, MODEL_WIDTH).astype(jnp.float32)
    chosen_down_matrix = shrink_matrices[block_table_rows].astype(jnp.float32)
    shrink = jnp.einsum('bnd,bdr->bnr', blocked, chosen_down_matrix)
    row_index = jnp.arange(BLOCK, dtype=jnp.int32)
    live = row_index[None, :] < token_rows_per_block[:, None]
    shrink = jnp.where(live[:, :, None], shrink, jnp.zeros_like(shrink)).astype(jnp.bfloat16)
    chosen_up_matrix = expand_matrices[block_table_rows].astype(jnp.float32)
    delta = jnp.einsum('bnr,brd->bnd', shrink.astype(jnp.float32), chosen_up_matrix).reshape(tokens, MODEL_WIDTH)
    return (base + delta).astype(jnp.bfloat16)
```

```python
import functools

import jax
import jax.numpy as jnp
from jax import lax
from jax.experimental import pallas as pl
from jax.experimental.pallas import tpu as pltpu
from jax.sharding import PartitionSpec as P

BLOCK = 128
CHUNK = 512
MESH = pl.DeviceIdType.MESH
F32 = jnp.float32
BF16 = jnp.bfloat16


def kernel(
    n,
    n_sp,
    n_ep,
    chunk,
    tenant_ref,
    live_ref,
    table_ref,
    x_hbm,
    w_hbm,
    a_hbm,
    b_hbm,
    o_hbm,
    x_v,
    w_v,
    prod,
    right,
    left,
    own,
    out_v,
    a_all,
    b_all,
    packs,
    lhs,
    x_sem,
    w_sem,
    right_send,
    right_recv,
    left_send,
    left_recv,
    a_local,
    a_send,
    a_recv,
    b_local,
    b_send,
    b_recv,
    pack_send,
    pack_recv,
    out_local,
    out_send,
    out_recv,
):
    z = lax.axis_index("tp")
    s = lax.axis_index("sp")
    e = lax.axis_index("ep")
    rows, depth = x_v.shape
    half = depth // 2
    width = o_hbm.shape[1]
    per = width // chunk
    blocks = rows // BLOCK
    pieces = a_hbm.shape[0]
    moving = (n - 1) * per
    row0 = pl.multiple_of(e * rows, BLOCK)

    x_copy = pltpu.make_async_copy(x_hbm.at[pl.ds(row0, rows), :], x_v, x_sem)
    x_copy.start()

    n_right = (n - 1 - z) * per
    n_left = z * per
    in_low = z < n // 2
    n_first = jnp.where(in_low, n_right, n_left)
    n_second = moving - n_first

    def item(i):
        paired = i <= 2 * n_second
        odd = i % 2
        index = jnp.where(
            paired,
            jnp.where(odd == 1, (i + 1) // 2, jnp.where(i == 0, 0, i // 2 - 1)),
            i - n_second,
        )
        second = jnp.where(paired & (odd == 0) & (i > 0), 1, 0)
        is_own = i >= moving
        goes_right = jnp.where(in_low, 1 - second, second)
        kind = jnp.where(is_own, 2, jnp.where(goes_right == 1, 0, 1))
        index = jnp.where(is_own, i - moving, index)
        return kind, index

    def column_of(i):
        kind, index = item(i)
        steps = index // per
        dest = jnp.where(kind == 2, z, jnp.where(kind == 0, n - 1 - steps, steps))
        return pl.multiple_of(dest * width + (index % per) * chunk, chunk)

    def w_copy(i):
        slot = i % 2
        return pltpu.make_async_copy(
            w_hbm.at[:, pl.ds(column_of(i), chunk)], w_v.at[slot], w_sem.at[slot]
        )

    w_copy(0).start()

    barrier = pltpu.get_barrier_semaphore()
    for k in range(1, n):
        pl.semaphore_signal(
            barrier, inc=1, device_id={"tp": lax.rem(z + k, n)}, device_id_type=MESH
        )
    for k in range(1, n_sp):
        pl.semaphore_signal(
            barrier, inc=1, device_id={"sp": lax.rem(s + k, n_sp)}, device_id_type=MESH
        )
    for k in range(1, n_ep):
        pl.semaphore_signal(
            barrier, inc=1, device_id={"ep": lax.rem(e + k, n_ep)}, device_id_type=MESH
        )
    pl.semaphore_wait(barrier, n + n_sp + n_ep - 3)

    sibling = {"ep": lax.rem(e + 1, n_ep)}

    def part(ref, owner_s, owner_e):
        start = (owner_s * n_ep + owner_e) * pieces
        return ref.at[pl.ds(start, pieces)]

    def along_sp(src, gathered, send, recv, k):
        return pltpu.make_async_remote_copy(
            src_ref=src,
            dst_ref=part(gathered, s, e),
            send_sem=send.at[k],
            recv_sem=recv.at[k],
            device_id={"sp": lax.rem(s + k, n_sp)},
            device_id_type=MESH,
        )

    def along_ep(src, gathered, send, recv, k):
        return pltpu.make_async_remote_copy(
            src_ref=src,
            dst_ref=part(gathered, lax.rem(s + n_sp - k, n_sp), e),
            send_sem=send.at[n_sp + k],
            recv_sem=recv.at[n_sp + k],
            device_id=sibling,
            device_id_type=MESH,
        )

    tables = (
        (a_hbm, a_all, a_local, a_send, a_recv),
        (b_hbm, b_all, b_local, b_send, b_recv),
    )

    def start_table(src, gathered, local, send, recv):
        for k in range(1, n_sp):
            along_sp(src, gathered, send, recv, k).start()
        along_ep(src, gathered, send, recv, 0).start()
        pltpu.make_async_copy(src, part(gathered, s, e), local).start()

    def forward_table(src, gathered, local, send, recv):
        for k in range(1, n_sp):
            along_sp(src, gathered, send, recv, k).wait_recv()
            piece = part(gathered, lax.rem(s + n_sp - k, n_sp), e)
            along_ep(piece, gathered, send, recv, k).start()

    def finish_table(src, gathered, local, send, recv):
        pltpu.make_async_copy(src, part(gathered, s, e), local).wait()
        for k in range(n_sp):
            along_ep(src, gathered, send, recv, k).wait_recv()

    def drain_table(src, gathered, local, send, recv):
        for k in range(1, n_sp):
            along_sp(src, gathered, send, recv, k).wait_send()
        for k in range(n_sp):
            along_ep(src, gathered, send, recv, k).wait_send()

    def right_copy(t):
        return pltpu.make_async_remote_copy(
            src_ref=right.at[t],
            dst_ref=right.at[t],
            send_sem=right_send.at[t],
            recv_sem=right_recv.at[t],
            device_id={"tp": z + 1},
            device_id_type=MESH,
        )

    def left_copy(t):
        return pltpu.make_async_remote_copy(
            src_ref=left.at[t],
            dst_ref=left.at[t],
            send_sem=left_send.at[t],
            recv_sem=left_recv.at[t],
            device_id={"tp": z - 1},
            device_id_type=MESH,
        )

    def step(i, carry):
        kind, t = item(i)
        slot = i % 2

        @pl.when(i + 1 < n * per)
        def _():
            w_copy(i + 1).start()

        w_copy(i).wait()
        prod[...] = jnp.dot(x_v[...], w_v[slot], preferred_element_type=F32)

        @pl.when(kind == 0)
        def _():
            @pl.when(z > 0)
            def _():
                right_copy(t).wait_recv()
                right[t] = (prod[...] + right[t].astype(F32)).astype(BF16)

            @pl.when(z == 0)
            def _():
                right[t] = prod[...].astype(BF16)

            right_copy(t).start()

        @pl.when(kind == 1)
        def _():
            @pl.when(z < n - 1)
            def _():
                left_copy(t).wait_recv()
                left[t] = (prod[...] + left[t].astype(F32)).astype(BF16)

            @pl.when(z == n - 1)
            def _():
                left[t] = prod[...].astype(BF16)

            left_copy(t).start()

        @pl.when(kind == 2)
        def _():
            own[t] = prod[...]

        return carry

    start_table(*tables[0])
    x_copy.wait()
    step(0, 0)
    start_table(*tables[1])
    turn_a = min(5, moving)
    turn_b = min(7, moving)
    lax.fori_loop(1, turn_a, step, 0)
    forward_table(*tables[0])
    lax.fori_loop(turn_a, turn_b, step, 0)
    finish_table(*tables[0])

    lane = lax.broadcasted_iota(jnp.int32, (BLOCK, 128), 1)
    rank = lane.shape[1] // 2

    def shrink_pair(b):
        slot = table_ref[tenant_ref[e * blocks + b]]
        rows_b = pl.ds(b * BLOCK, BLOCK)
        matrix = a_all[slot]
        low = jnp.dot(x_v[rows_b, :half], matrix, preferred_element_type=F32)
        high = jnp.dot(x_v[rows_b, half:], matrix, preferred_element_type=F32)
        return low, high

    for p in range(blocks // 2):
        low, high = shrink_pair(2 * p)
        low2, high2 = shrink_pair(2 * p + 1)
        both = jnp.where(
            lane < rank,
            low + pltpu.roll(high, rank, 1),
            pltpu.roll(low2, rank, 1) + high2,
        )
        packs[0, p] = both.astype(BF16)

    def pack_copy(k):
        return pltpu.make_async_remote_copy(
            src_ref=packs.at[0],
            dst_ref=packs.at[k],
            send_sem=pack_send.at[k],
            recv_sem=pack_recv.at[k],
            device_id={"tp": lax.rem(z + k, n)},
            device_id_type=MESH,
        )

    for k in range(1, n):
        pack_copy(k).start()

    lax.fori_loop(turn_b, n * per, step, 0)
    forward_table(*tables[1])

    for k in range(1, n):
        pack_copy(k).wait_recv()
    row = lax.broadcasted_iota(jnp.int32, (BLOCK, 128), 0)
    for p in range(blocks // 2):
        total = packs[0, p].astype(F32)
        for k in range(1, n):
            total = total + packs[k, p].astype(F32)
        for side in range(2):
            b = 2 * p + side
            mine = (lane < rank) if side == 0 else (lane >= rank)
            keep = mine & (row < live_ref[e * blocks + b])
            lhs[b] = jnp.where(keep, total, 0.0).astype(BF16)

    finish_table(*tables[1])
    for b in range(blocks):
        slot = table_ref[tenant_ref[e * blocks + b]]
        matrix = b_all[slot]
        stacked = jnp.concatenate([matrix, matrix], axis=0)
        for j in range(per):
            own[j, b * BLOCK : (b + 1) * BLOCK, :] += jnp.dot(
                lhs[b],
                stacked[:, j * chunk : (j + 1) * chunk],
                preferred_element_type=F32,
            )

    def out_place(j):
        return o_hbm.at[pl.ds(row0, rows), pl.ds(j * chunk, chunk)]

    def out_remote(j):
        return pltpu.make_async_remote_copy(
            src_ref=out_v.at[j],
            dst_ref=out_place(j),
            send_sem=out_send.at[j],
            recv_sem=out_recv.at[j],
            device_id=sibling,
            device_id_type=MESH,
        )

    for j in range(per):
        @pl.when(z < n - 1)
        def _():
            t = z * per + j
            left_copy(t).wait_recv()
            own[j] += left[t].astype(F32)

        @pl.when(z > 0)
        def _():
            t = (n - 1 - z) * per + j
            right_copy(t).wait_recv()
            own[j] += right[t].astype(F32)

        out_v[j] = own[j].astype(BF16)
        out_remote(j).start()
        pltpu.make_async_copy(out_v.at[j], out_place(j), out_local.at[j]).start()

    def right_done(t, carry):
        right_copy(t).wait_send()
        return carry

    def left_done(t, carry):
        left_copy(t).wait_send()
        return carry

    lax.fori_loop(0, n_right, right_done, 0)
    lax.fori_loop(0, n_left, left_done, 0)
    drain_table(*tables[0])
    drain_table(*tables[1])
    for k in range(1, n):
        pack_copy(k).wait_send()
    for j in range(per):
        out_remote(j).wait()
        pltpu.make_async_copy(out_v.at[j], out_place(j), out_local.at[j]).wait()


def per_device(
    n,
    n_sp,
    n_ep,
    activations,
    output_projection_weight,
    shrink_matrices,
    expand_matrices,
    tenant_of_block,
    token_rows_per_block,
    tenant_table_row,
):
    all_rows, depth = activations.shape
    rows = all_rows // n_ep
    width = expand_matrices.shape[2]
    chunk = min(CHUNK, width)
    per = width // chunk
    blocks = rows // BLOCK
    pieces, _, rank = shrink_matrices.shape
    count = pieces * n_sp * n_ep
    folded = jnp.concatenate(
        [shrink_matrices[:, : depth // 2], shrink_matrices[:, depth // 2 :]], axis=2
    )
    moving = (n - 1) * per
    dma = pltpu.SemaphoreType.DMA
    smem = pl.BlockSpec(memory_space=pltpu.SMEM)
    anywhere = pl.BlockSpec(memory_space=pl.ANY)
    return pl.pallas_call(
        functools.partial(kernel, n, n_sp, n_ep, chunk),
        out_shape=jax.ShapeDtypeStruct((all_rows, width), BF16),
        in_specs=[smem, smem, smem, anywhere, anywhere, anywhere, anywhere],
        out_specs=anywhere,
        scratch_shapes=[
            pltpu.VMEM((rows, depth), BF16),
            pltpu.VMEM((2, depth, chunk), BF16),
            pltpu.VMEM((rows, chunk), F32),
            pltpu.VMEM((moving, rows, chunk), BF16),
            pltpu.VMEM((moving, rows, chunk), BF16),
            pltpu.VMEM((per, rows, chunk), F32),
            pltpu.VMEM((per, rows, chunk), BF16),
            pltpu.VMEM((count, depth // 2, 2 * rank), BF16),
            pltpu.VMEM((count, rank, width), BF16),
            pltpu.VMEM((n, blocks // 2, BLOCK, 2 * rank), BF16),
            pltpu.VMEM((blocks, BLOCK, 2 * rank), BF16),
            dma,
            dma((2,)),
            dma((moving,)),
            dma((moving,)),
            dma((moving,)),
            dma((moving,)),
            dma,
            dma((2 * n_sp,)),
            dma((2 * n_sp,)),
            dma,
            dma((2 * n_sp,)),
            dma((2 * n_sp,)),
            dma((n,)),
            dma((n,)),
            dma((per,)),
            dma((per,)),
            dma((per,)),
        ],
        compiler_params=pltpu.CompilerParams(
            collective_id=0,
            has_side_effects=True,
            vmem_limit_bytes=56 * 1024 * 1024,
        ),
    )(
        tenant_of_block,
        token_rows_per_block,
        tenant_table_row,
        activations,
        output_projection_weight,
        folded,
        expand_matrices,
    )


def solution(mesh):
    in_specs = (
        P(("groups", "sp"), "tp"),
        P("tp", None),
        P(("sp", "ep"), "tp", None),
        P(("sp", "ep"), None, "tp"),
        P(("groups", "sp")),
        P(("groups", "sp")),
        P(),
    )
    return jax.shard_map(
        functools.partial(
            per_device, mesh.shape["tp"], mesh.shape["sp"], mesh.shape["ep"]
        ),
        mesh=mesh,
        in_specs=in_specs,
        out_specs=P(("groups", "sp"), "tp"),
        check_vma=False,
    )
```

```python
import functools

import jax
import jax.numpy as jnp
from jax import lax
from jax.experimental import pallas as pl
from jax.experimental.pallas import tpu as pltpu
from jax.sharding import PartitionSpec as P

BLOCK = 128
CHUNK = 256
MESH = pl.DeviceIdType.MESH
F32 = jnp.float32
BF16 = jnp.bfloat16


def kernel(
    n,
    n_sp,
    n_ep,
    chunk,
    tenant_ref,
    live_ref,
    table_ref,
    x_hbm,
    w_hbm,
    a_hbm,
    b_hbm,
    o_ref,
    x_v,
    w_v,
    prod,
    right,
    left,
    own,
    a_all,
    b_all,
    packs,
    from_left,
    from_right,
    pack_right,
    pack_left,
    lhs,
    x_sem,
    w_sem,
    right_send,
    right_recv,
    left_send,
    left_recv,
    a_local,
    a_send,
    a_recv,
    b_local,
    b_send,
    b_recv,
    pack_send,
    pack_recv,
    out_send,
    out_recv,
):
    z = lax.axis_index("tp")
    s = lax.axis_index("sp")
    e = lax.axis_index("ep")
    rows = x_v.shape[0]
    width = o_ref.shape[1]
    per = width // chunk
    blocks = rows // BLOCK
    pieces = a_hbm.shape[0]
    moving = (n - 1) * per
    row0 = pl.multiple_of(e * rows, BLOCK)

    x_copy = pltpu.make_async_copy(x_hbm.at[pl.ds(row0, rows), :], x_v, x_sem)
    x_copy.start()

    n_right = (n - 1 - z) * per
    n_left = z * per
    in_low = z < n // 2
    n_first = jnp.where(in_low, n_right, n_left)
    n_second = moving - n_first

    def item(i):
        paired = i <= 2 * n_second
        odd = i % 2
        index = jnp.where(
            paired,
            jnp.where(odd == 1, (i + 1) // 2, jnp.where(i == 0, 0, i // 2 - 1)),
            i - n_second,
        )
        second = jnp.where(paired & (odd == 0) & (i > 0), 1, 0)
        is_own = i >= moving
        goes_right = jnp.where(in_low, 1 - second, second)
        kind = jnp.where(is_own, 2, jnp.where(goes_right == 1, 0, 1))
        index = jnp.where(is_own, i - moving, index)
        return kind, index

    def column_of(i):
        kind, index = item(i)
        steps = index // per
        dest = jnp.where(kind == 2, z, jnp.where(kind == 0, n - 1 - steps, steps))
        return pl.multiple_of(dest * width + (index % per) * chunk, chunk)

    def w_copy(i):
        slot = i % 2
        return pltpu.make_async_copy(
            w_hbm.at[:, pl.ds(column_of(i), chunk)], w_v.at[slot], w_sem.at[slot]
        )

    w_copy(0).start()

    barrier = pltpu.get_barrier_semaphore()
    for k in range(1, n):
        pl.semaphore_signal(
            barrier, inc=1, device_id={"tp": lax.rem(z + k, n)}, device_id_type=MESH
        )
    for k in range(1, n_sp):
        pl.semaphore_signal(
            barrier, inc=1, device_id={"sp": lax.rem(s + k, n_sp)}, device_id_type=MESH
        )
    for k in range(1, n_ep):
        pl.semaphore_signal(
            barrier, inc=1, device_id={"ep": lax.rem(e + k, n_ep)}, device_id_type=MESH
        )
    pl.semaphore_wait(barrier, n + n_sp + n_ep - 3)

    sibling = {"ep": lax.rem(e + 1, n_ep)}

    def part(ref, owner_s, owner_e):
        start = (owner_s * n_ep + owner_e) * pieces
        return ref.at[pl.ds(start, pieces)]

    def along_sp(src, gathered, send, recv, k):
        return pltpu.make_async_remote_copy(
            src_ref=src,
            dst_ref=part(gathered, s, e),
            send_sem=send.at[k],
            recv_sem=recv.at[k],
            device_id={"sp": lax.rem(s + k, n_sp)},
            device_id_type=MESH,
        )

    def along_ep(src, gathered, send, recv, k):
        return pltpu.make_async_remote_copy(
            src_ref=src,
            dst_ref=part(gathered, lax.rem(s + n_sp - k, n_sp), e),
            send_sem=send.at[n_sp + k],
            recv_sem=recv.at[n_sp + k],
            device_id=sibling,
            device_id_type=MESH,
        )

    tables = (
        (a_hbm, a_all, a_local, a_send, a_recv),
        (b_hbm, b_all, b_local, b_send, b_recv),
    )

    def start_table(src, gathered, local, send, recv):
        for k in range(1, n_sp):
            along_sp(src, gathered, send, recv, k).start()
        along_ep(src, gathered, send, recv, 0).start()
        pltpu.make_async_copy(src, part(gathered, s, e), local).start()

    def forward_table(src, gathered, local, send, recv):
        for k in range(1, n_sp):
            along_sp(src, gathered, send, recv, k).wait_recv()
            piece = part(gathered, lax.rem(s + n_sp - k, n_sp), e)
            along_ep(piece, gathered, send, recv, k).start()

    def finish_table(src, gathered, local, send, recv):
        pltpu.make_async_copy(src, part(gathered, s, e), local).wait()
        for k in range(n_sp):
            along_ep(src, gathered, send, recv, k).wait_recv()

    def drain_table(src, gathered, local, send, recv):
        for k in range(1, n_sp):
            along_sp(src, gathered, send, recv, k).wait_send()
        for k in range(n_sp):
            along_ep(src, gathered, send, recv, k).wait_send()

    def right_copy(t):
        return pltpu.make_async_remote_copy(
            src_ref=right.at[t],
            dst_ref=right.at[t],
            send_sem=right_send.at[t],
            recv_sem=right_recv.at[t],
            device_id={"tp": z + 1},
            device_id_type=MESH,
        )

    def left_copy(t):
        return pltpu.make_async_remote_copy(
            src_ref=left.at[t],
            dst_ref=left.at[t],
            send_sem=left_send.at[t],
            recv_sem=left_recv.at[t],
            device_id={"tp": z - 1},
            device_id_type=MESH,
        )

    def pack_right_copy():
        return pltpu.make_async_remote_copy(
            src_ref=pack_right,
            dst_ref=pack_right,
            send_sem=pack_send.at[0],
            recv_sem=pack_recv.at[0],
            device_id={"tp": z + 1},
            device_id_type=MESH,
        )

    def pack_left_copy():
        return pltpu.make_async_remote_copy(
            src_ref=pack_left,
            dst_ref=pack_left,
            send_sem=pack_send.at[1],
            recv_sem=pack_recv.at[1],
            device_id={"tp": z - 1},
            device_id_type=MESH,
        )

    def step(i, carry):
        kind, t = item(i)
        slot = i % 2

        @pl.when(i + 1 < n * per)
        def _():
            w_copy(i + 1).start()

        w_copy(i).wait()
        prod[...] = jnp.dot(x_v[...], w_v[slot], preferred_element_type=F32)

        @pl.when(kind == 0)
        def _():
            @pl.when(z > 0)
            def _():
                right_copy(t).wait_recv()
                right[t] = (prod[...] + right[t].astype(F32)).astype(BF16)

            @pl.when(z == 0)
            def _():
                right[t] = prod[...].astype(BF16)

            right_copy(t).start()

        @pl.when(kind == 1)
        def _():
            @pl.when(z < n - 1)
            def _():
                left_copy(t).wait_recv()
                left[t] = (prod[...] + left[t].astype(F32)).astype(BF16)

            @pl.when(z == n - 1)
            def _():
                left[t] = prod[...].astype(BF16)

            left_copy(t).start()

        @pl.when(kind == 2)
        def _():
            own[t] = prod[...]

        return carry

    x_copy.wait()
    step(0, 0)
    start_table(*tables[0])
    start_table(*tables[1])
    turn_a = max(1, moving * 5 // 12)
    turn_b = max(1, moving * 7 // 12)
    lax.fori_loop(1, turn_a, step, 0)
    forward_table(*tables[0])
    lax.fori_loop(turn_a, turn_b, step, 0)
    finish_table(*tables[0])

    rank = b_hbm.shape[1]
    lane = lax.broadcasted_iota(jnp.int32, (BLOCK, 2 * rank), 1)

    def shrink_twice(b):
        slot = table_ref[tenant_ref[e * blocks + b]]
        matrix = a_all[slot]
        return lax.dot_general(
            x_v[b * BLOCK : (b + 1) * BLOCK, :],
            jnp.concatenate([matrix, matrix], axis=0),
            (((1,), (1,)), ((), ())),
            preferred_element_type=F32,
        )

    for p in range(blocks // 2):
        packs[p] = jnp.where(
            lane < rank, shrink_twice(2 * p), shrink_twice(2 * p + 1)
        )

    @pl.when(z == 0)
    def _():
        pack_right[...] = packs[...].astype(BF16)
        pack_right_copy().start()

    @pl.when(z == n - 1)
    def _():
        pack_left[...] = packs[...].astype(BF16)
        pack_left_copy().start()

    lax.fori_loop(turn_b, moving, step, 0)

    def pass_right():
        @pl.when(z > 0)
        def _():
            pack_right_copy().wait_recv()
            from_left[...] = pack_right[...].astype(F32)

            @pl.when(z < n - 1)
            def _():
                pack_right[...] = (packs[...] + from_left[...]).astype(BF16)
                pack_right_copy().start()

    def pass_left():
        @pl.when(z < n - 1)
        def _():
            pack_left_copy().wait_recv()
            from_right[...] = pack_left[...].astype(F32)

            @pl.when(z > 0)
            def _():
                pack_left[...] = (packs[...] + from_right[...]).astype(BF16)
                pack_left_copy().start()

    from_left[...] = jnp.zeros_like(from_left)
    from_right[...] = jnp.zeros_like(from_right)

    @pl.when(in_low)
    def _():
        pass_right()

    pass_left()

    @pl.when(jnp.logical_not(in_low))
    def _():
        pass_right()

    lax.fori_loop(moving, n * per, step, 0)
    forward_table(*tables[1])

    row = lax.broadcasted_iota(jnp.int32, (BLOCK, 2 * rank), 0)
    for p in range(blocks // 2):
        total = packs[p] + from_left[p] + from_right[p]
        for side in range(2):
            b = 2 * p + side
            mine = (lane < rank) if side == 0 else (lane >= rank)
            keep = mine & (row < live_ref[e * blocks + b])
            lhs[b] = jnp.where(keep, total, 0.0).astype(BF16)

    finish_table(*tables[1])
    for b in range(blocks):
        slot = table_ref[tenant_ref[e * blocks + b]]
        matrix = b_all[slot]
        stacked = jnp.concatenate([matrix, matrix], axis=0)
        for j in range(per):
            own[j, b * BLOCK : (b + 1) * BLOCK, :] += jnp.dot(
                lhs[b],
                stacked[:, j * chunk : (j + 1) * chunk],
                preferred_element_type=F32,
            )

    def out_remote(j):
        place = o_ref.at[pl.ds(row0, rows), pl.ds(j * chunk, chunk)]
        return pltpu.make_async_remote_copy(
            src_ref=place,
            dst_ref=place,
            send_sem=out_send.at[j],
            recv_sem=out_recv.at[j],
            device_id=sibling,
            device_id_type=MESH,
        )

    for j in range(per):
        @pl.when(z < n - 1)
        def _():
            t = z * per + j
            left_copy(t).wait_recv()
            own[j] += left[t].astype(F32)

        @pl.when(z > 0)
        def _():
            t = (n - 1 - z) * per + j
            right_copy(t).wait_recv()
            own[j] += right[t].astype(F32)

        o_ref[pl.ds(row0, rows), j * chunk : (j + 1) * chunk] = own[j].astype(BF16)
        out_remote(j).start()

    def right_done(t, carry):
        right_copy(t).wait_send()
        return carry

    def left_done(t, carry):
        left_copy(t).wait_send()
        return carry

    lax.fori_loop(0, n_right, right_done, 0)
    lax.fori_loop(0, n_left, left_done, 0)
    drain_table(*tables[0])
    drain_table(*tables[1])

    @pl.when(z < n - 1)
    def _():
        pack_right_copy().wait_send()

    @pl.when(z > 0)
    def _():
        pack_left_copy().wait_send()

    for j in range(per):
        out_remote(j).wait()


def per_device(
    n,
    n_sp,
    n_ep,
    activations,
    output_projection_weight,
    shrink_matrices,
    expand_matrices,
    tenant_of_block,
    token_rows_per_block,
    tenant_table_row,
):
    all_rows, depth = activations.shape
    rows = all_rows // n_ep
    width = expand_matrices.shape[2]
    chunk = min(CHUNK, width)
    per = width // chunk
    blocks = rows // BLOCK
    pieces, _, rank = shrink_matrices.shape
    count = pieces * n_sp * n_ep
    turned = jnp.swapaxes(shrink_matrices, 1, 2)
    pack = (blocks // 2, BLOCK, 2 * rank)
    moving = (n - 1) * per
    dma = pltpu.SemaphoreType.DMA
    smem = pl.BlockSpec(memory_space=pltpu.SMEM)
    anywhere = pl.BlockSpec(memory_space=pl.ANY)
    return pl.pallas_call(
        functools.partial(kernel, n, n_sp, n_ep, chunk),
        out_shape=pltpu.VMEM((all_rows, width), BF16),
        in_specs=[smem, smem, smem, anywhere, anywhere, anywhere, anywhere],
        out_specs=pl.BlockSpec(memory_space=pltpu.VMEM),
        scratch_shapes=[
            pltpu.VMEM((rows, depth), BF16),
            pltpu.VMEM((2, depth, chunk), BF16),
            pltpu.VMEM((rows, chunk), F32),
            pltpu.VMEM((moving, rows, chunk), BF16),
            pltpu.VMEM((moving, rows, chunk), BF16),
            pltpu.VMEM((per, rows, chunk), F32),
            pltpu.VMEM((count, rank, depth), BF16),
            pltpu.VMEM((count, rank, width), BF16),
            pltpu.VMEM(pack, F32),
            pltpu.VMEM(pack, F32),
            pltpu.VMEM(pack, F32),
            pltpu.VMEM(pack, BF16),
            pltpu.VMEM(pack, BF16),
            pltpu.VMEM((blocks, BLOCK, 2 * rank), BF16),
            dma,
            dma((2,)),
            dma((moving,)),
            dma((moving,)),
            dma((moving,)),
            dma((moving,)),
            dma,
            dma((2 * n_sp,)),
            dma((2 * n_sp,)),
            dma,
            dma((2 * n_sp,)),
            dma((2 * n_sp,)),
            dma((2,)),
            dma((2,)),
            dma((per,)),
            dma((per,)),
        ],
        compiler_params=pltpu.CompilerParams(
            collective_id=0,
            has_side_effects=True,
            vmem_limit_bytes=48 * 1024 * 1024,
        ),
    )(
        tenant_of_block,
        token_rows_per_block,
        tenant_table_row,
        activations,
        output_projection_weight,
        turned,
        expand_matrices,
    )


def solution(mesh):
    in_specs = (
        P(("groups", "sp"), "tp"),
        P("tp", None),
        P(("sp", "ep"), "tp", None),
        P(("sp", "ep"), None, "tp"),
        P(("groups", "sp")),
        P(("groups", "sp")),
        P(),
    )
    return jax.shard_map(
        functools.partial(
            per_device, mesh.shape["tp"], mesh.shape["sp"], mesh.shape["ep"]
        ),
        mesh=mesh,
        in_specs=in_specs,
        out_specs=P(("groups", "sp"), "tp"),
        check_vma=False,
    )
```

```python
import functools

import jax
import jax.numpy as jnp
from jax import lax
from jax.experimental import pallas as pl
from jax.experimental.pallas import tpu as pltpu
from jax.sharding import PartitionSpec as P

BLOCK = 128
CHUNK = 256
MESH = pl.DeviceIdType.MESH
F32 = jnp.float32
BF16 = jnp.bfloat16


def kernel(
    n,
    n_sp,
    n_ep,
    chunk,
    tenant_hbm,
    live_hbm,
    table_hbm,
    x_hbm,
    w_hbm,
    a_hbm,
    b_hbm,
    o_ref,
    tenant_ref,
    live_ref,
    table_ref,
    x_v,
    w_v,
    prod,
    right,
    left,
    own,
    a_all,
    b_all,
    packs,
    from_left,
    from_right,
    pack_right,
    pack_left,
    lhs,
    int_sem,
    x_sem,
    w_sem,
    right_send,
    right_recv,
    left_send,
    left_recv,
    a_local,
    a_send,
    a_recv,
    b_local,
    b_send,
    b_recv,
    pack_send,
    pack_recv,
    out_send,
    out_recv,
):
    z = lax.axis_index("tp")
    s = lax.axis_index("sp")
    e = lax.axis_index("ep")
    rows = x_v.shape[0]
    width = o_ref.shape[1]
    per = width // chunk
    blocks = rows // BLOCK
    pieces = a_hbm.shape[0]
    moving = (n - 1) * per
    row0 = pl.multiple_of(e * rows, BLOCK)

    x_copy = pltpu.make_async_copy(x_hbm.at[pl.ds(row0, rows), :], x_v, x_sem)
    x_copy.start()

    n_right = (n - 1 - z) * per
    n_left = z * per
    in_low = z < n // 2
    n_first = jnp.where(in_low, n_right, n_left)
    n_second = moving - n_first

    def item(i):
        paired = i <= 2 * n_second
        odd = i % 2
        index = jnp.where(
            paired,
            jnp.where(odd == 1, (i + 1) // 2, jnp.where(i == 0, 0, i // 2 - 1)),
            i - n_second,
        )
        second = jnp.where(paired & (odd == 0) & (i > 0), 1, 0)
        is_own = i >= moving
        goes_right = jnp.where(in_low, 1 - second, second)
        kind = jnp.where(is_own, 2, jnp.where(goes_right == 1, 0, 1))
        index = jnp.where(is_own, i - moving, index)
        return kind, index

    def column_of(i):
        kind, index = item(i)
        steps = index // per
        dest = jnp.where(kind == 2, z, jnp.where(kind == 0, n - 1 - steps, steps))
        return pl.multiple_of(dest * width + (index % per) * chunk, chunk)

    def w_copy(i):
        slot = i % 2
        return pltpu.make_async_copy(
            w_hbm.at[:, pl.ds(column_of(i), chunk)], w_v.at[slot], w_sem.at[slot]
        )

    w_copy(0).start()

    int_copies = [
        pltpu.make_async_copy(src, dst, int_sem.at[k])
        for k, (src, dst) in enumerate(
            ((tenant_hbm, tenant_ref), (live_hbm, live_ref), (table_hbm, table_ref))
        )
    ]

    barrier = pltpu.get_barrier_semaphore()

    def greet(device_id):
        pl.semaphore_signal(barrier, inc=1, device_id=device_id, device_id_type=MESH)

    @pl.when(z > 0)
    def _():
        greet({"tp": z - 1})

    @pl.when(z < n - 1)
    def _():
        greet({"tp": z + 1})

    for k in range(1, n_sp):
        greet({"sp": lax.rem(s + k, n_sp)})
    for k in range(1, n_ep):
        greet({"ep": lax.rem(e + k, n_ep)})
    along_line = jnp.where(z > 0, 1, 0) + jnp.where(z < n - 1, 1, 0)
    greeters = along_line + (n_sp - 1) + (n_ep - 1)

    sibling = {"ep": lax.rem(e + 1, n_ep)}

    def part(ref, owner_s, owner_e):
        start = (owner_s * n_ep + owner_e) * pieces
        return ref.at[pl.ds(start, pieces)]

    def along_sp(src, gathered, send, recv, k):
        return pltpu.make_async_remote_copy(
            src_ref=src,
            dst_ref=part(gathered, s, e),
            send_sem=send.at[k],
            recv_sem=recv.at[k],
            device_id={"sp": lax.rem(s + k, n_sp)},
            device_id_type=MESH,
        )

    def along_ep(src, gathered, send, recv, k):
        return pltpu.make_async_remote_copy(
            src_ref=src,
            dst_ref=part(gathered, lax.rem(s + n_sp - k, n_sp), e),
            send_sem=send.at[n_sp + k],
            recv_sem=recv.at[n_sp + k],
            device_id=sibling,
            device_id_type=MESH,
        )

    tables = (
        (a_hbm, a_all, a_local, a_send, a_recv),
        (b_hbm, b_all, b_local, b_send, b_recv),
    )

    def start_table(src, gathered, local, send, recv):
        for k in range(1, n_sp):
            along_sp(src, gathered, send, recv, k).start()
        along_ep(src, gathered, send, recv, 0).start()
        pltpu.make_async_copy(src, part(gathered, s, e), local).start()

    def forward_table(src, gathered, local, send, recv):
        for k in range(1, n_sp):
            along_sp(src, gathered, send, recv, k).wait_recv()
            piece = part(gathered, lax.rem(s + n_sp - k, n_sp), e)
            along_ep(piece, gathered, send, recv, k).start()

    def finish_table(src, gathered, local, send, recv):
        pltpu.make_async_copy(src, part(gathered, s, e), local).wait()
        for k in range(n_sp):
            along_ep(src, gathered, send, recv, k).wait_recv()

    def drain_table(src, gathered, local, send, recv):
        for k in range(1, n_sp):
            along_sp(src, gathered, send, recv, k).wait_send()
        for k in range(n_sp):
            along_ep(src, gathered, send, recv, k).wait_send()

    def right_copy(t):
        return pltpu.make_async_remote_copy(
            src_ref=right.at[t],
            dst_ref=right.at[t],
            send_sem=right_send.at[t],
            recv_sem=right_recv.at[t],
            device_id={"tp": z + 1},
            device_id_type=MESH,
        )

    def left_copy(t):
        return pltpu.make_async_remote_copy(
            src_ref=left.at[t],
            dst_ref=left.at[t],
            send_sem=left_send.at[t],
            recv_sem=left_recv.at[t],
            device_id={"tp": z - 1},
            device_id_type=MESH,
        )

    def pack_right_copy():
        return pltpu.make_async_remote_copy(
            src_ref=pack_right,
            dst_ref=pack_right,
            send_sem=pack_send.at[0],
            recv_sem=pack_recv.at[0],
            device_id={"tp": z + 1},
            device_id_type=MESH,
        )

    def pack_left_copy():
        return pltpu.make_async_remote_copy(
            src_ref=pack_left,
            dst_ref=pack_left,
            send_sem=pack_send.at[1],
            recv_sem=pack_recv.at[1],
            device_id={"tp": z - 1},
            device_id_type=MESH,
        )

    def multiply(i):
        slot = i % 2

        @pl.when(i + 1 < n * per)
        def _():
            w_copy(i + 1).start()

        w_copy(i).wait()
        prod[...] = jnp.dot(x_v[...], w_v[slot], preferred_element_type=F32)

    def pass_on(i):
        kind, t = item(i)

        @pl.when(kind == 0)
        def _():
            @pl.when(z > 0)
            def _():
                right_copy(t).wait_recv()
                right[t] = (prod[...] + right[t].astype(F32)).astype(BF16)

            @pl.when(z == 0)
            def _():
                right[t] = prod[...].astype(BF16)

            right_copy(t).start()

        @pl.when(kind == 1)
        def _():
            @pl.when(z < n - 1)
            def _():
                left_copy(t).wait_recv()
                left[t] = (prod[...] + left[t].astype(F32)).astype(BF16)

            @pl.when(z == n - 1)
            def _():
                left[t] = prod[...].astype(BF16)

            left_copy(t).start()

        @pl.when(kind == 2)
        def _():
            own[t] = prod[...]

    def step(i, carry):
        multiply(i)
        pass_on(i)
        return carry

    x_copy.wait()
    multiply(0)
    pl.semaphore_wait(barrier, greeters)
    pass_on(0)
    start_table(*tables[0])
    start_table(*tables[1])
    for copy in int_copies:
        copy.start()
    turn_a = max(1, moving * 5 // 12)
    turn_b = max(1, moving * 7 // 12)
    lax.fori_loop(1, turn_a, step, 0)
    forward_table(*tables[0])
    lax.fori_loop(turn_a, turn_b, step, 0)
    finish_table(*tables[0])
    for copy in int_copies:
        copy.wait()

    rank = b_hbm.shape[1]
    lane = lax.broadcasted_iota(jnp.int32, (BLOCK, 2 * rank), 1)

    def shrink_twice(b):
        slot = table_ref[tenant_ref[e * blocks + b]]
        matrix = a_all[slot]
        return lax.dot_general(
            x_v[b * BLOCK : (b + 1) * BLOCK, :],
            jnp.concatenate([matrix, matrix], axis=0),
            (((1,), (1,)), ((), ())),
            preferred_element_type=F32,
        )

    for p in range(blocks // 2):
        packs[p] = jnp.where(
            lane < rank, shrink_twice(2 * p), shrink_twice(2 * p + 1)
        )

    @pl.when(z == 0)
    def _():
        pack_right[...] = packs[...].astype(BF16)
        pack_right_copy().start()

    @pl.when(z == n - 1)
    def _():
        pack_left[...] = packs[...].astype(BF16)
        pack_left_copy().start()

    lax.fori_loop(turn_b, moving, step, 0)

    def pass_right():
        @pl.when(z > 0)
        def _():
            pack_right_copy().wait_recv()
            from_left[...] = pack_right[...].astype(F32)

            @pl.when(z < n - 1)
            def _():
                pack_right[...] = (packs[...] + from_left[...]).astype(BF16)
                pack_right_copy().start()

    def pass_left():
        @pl.when(z < n - 1)
        def _():
            pack_left_copy().wait_recv()
            from_right[...] = pack_left[...].astype(F32)

            @pl.when(z > 0)
            def _():
                pack_left[...] = (packs[...] + from_right[...]).astype(BF16)
                pack_left_copy().start()

    from_left[...] = jnp.zeros_like(from_left)
    from_right[...] = jnp.zeros_like(from_right)

    @pl.when(in_low)
    def _():
        pass_right()

    pass_left()

    @pl.when(jnp.logical_not(in_low))
    def _():
        pass_right()

    lax.fori_loop(moving, n * per, step, 0)
    forward_table(*tables[1])

    row = lax.broadcasted_iota(jnp.int32, (BLOCK, 2 * rank), 0)
    for p in range(blocks // 2):
        total = packs[p] + from_left[p] + from_right[p]
        for side in range(2):
            b = 2 * p + side
            mine = (lane < rank) if side == 0 else (lane >= rank)
            keep = mine & (row < live_ref[e * blocks + b])
            lhs[b] = jnp.where(keep, total, 0.0).astype(BF16)

    finish_table(*tables[1])
    for b in range(blocks):
        slot = table_ref[tenant_ref[e * blocks + b]]
        matrix = b_all[slot]
        stacked = jnp.concatenate([matrix, matrix], axis=0)
        for j in range(per):
            own[j, b * BLOCK : (b + 1) * BLOCK, :] += jnp.dot(
                lhs[b],
                stacked[:, j * chunk : (j + 1) * chunk],
                preferred_element_type=F32,
            )

    def out_remote(j):
        place = o_ref.at[pl.ds(row0, rows), pl.ds(j * chunk, chunk)]
        return pltpu.make_async_remote_copy(
            src_ref=place,
            dst_ref=place,
            send_sem=out_send.at[j],
            recv_sem=out_recv.at[j],
            device_id=sibling,
            device_id_type=MESH,
        )

    def take_left(j):
        left_copy(z * per + j).wait_recv()
        return left[z * per + j].astype(F32)

    def take_right(j):
        t = (n - 1 - z) * per + j
        right_copy(t).wait_recv()
        return right[t].astype(F32)

    def finish(j, value):
        o_ref[pl.ds(row0, rows), j * chunk : (j + 1) * chunk] = value.astype(BF16)
        out_remote(j).start()

    @pl.when(in_low)
    def _():
        for j in range(per):
            own[j] += take_left(j)

        @pl.when(z > 0)
        def _():
            for j in range(per):
                finish(j, own[j] + take_right(j))

    @pl.when(jnp.logical_not(in_low))
    def _():
        for j in range(per):
            own[j] += take_right(j)

        @pl.when(z < n - 1)
        def _():
            for j in range(per):
                finish(j, own[j] + take_left(j))

    @pl.when((z == 0) | (z == n - 1))
    def _():
        for j in range(per):
            finish(j, own[j])

    def right_done(t, carry):
        right_copy(t).wait_send()
        return carry

    def left_done(t, carry):
        left_copy(t).wait_send()
        return carry

    lax.fori_loop(0, n_right, right_done, 0)
    lax.fori_loop(0, n_left, left_done, 0)
    drain_table(*tables[0])
    drain_table(*tables[1])

    @pl.when(z < n - 1)
    def _():
        pack_right_copy().wait_send()

    @pl.when(z > 0)
    def _():
        pack_left_copy().wait_send()

    for j in range(per):
        out_remote(j).wait()


def per_device(
    n,
    n_sp,
    n_ep,
    activations,
    output_projection_weight,
    shrink_matrices,
    expand_matrices,
    tenant_of_block,
    token_rows_per_block,
    tenant_table_row,
):
    all_rows, depth = activations.shape
    rows = all_rows // n_ep
    width = expand_matrices.shape[2]
    chunk = min(CHUNK, width)
    per = width // chunk
    blocks = rows // BLOCK
    pieces, _, rank = shrink_matrices.shape
    count = pieces * n_sp * n_ep
    turned = jnp.swapaxes(shrink_matrices, 1, 2)
    pack = (blocks // 2, BLOCK, 2 * rank)
    moving = (n - 1) * per
    dma = pltpu.SemaphoreType.DMA
    in_hbm = pl.BlockSpec(memory_space=pltpu.HBM)
    return pl.pallas_call(
        functools.partial(kernel, n, n_sp, n_ep, chunk),
        out_shape=pltpu.VMEM((all_rows, width), BF16),
        in_specs=[in_hbm] * 7,
        out_specs=pl.BlockSpec(memory_space=pltpu.VMEM),
        scratch_shapes=[
            pltpu.SMEM(tenant_of_block.shape, jnp.int32),
            pltpu.SMEM(token_rows_per_block.shape, jnp.int32),
            pltpu.SMEM(tenant_table_row.shape, jnp.int32),
            pltpu.VMEM((rows, depth), BF16),
            pltpu.VMEM((2, depth, chunk), BF16),
            pltpu.VMEM((rows, chunk), F32),
            pltpu.VMEM((moving, rows, chunk), BF16),
            pltpu.VMEM((moving, rows, chunk), BF16),
            pltpu.VMEM((per, rows, chunk), F32),
            pltpu.VMEM((count, rank, depth), BF16),
            pltpu.VMEM((count, rank, width), BF16),
            pltpu.VMEM(pack, F32),
            pltpu.VMEM(pack, F32),
            pltpu.VMEM(pack, F32),
            pltpu.VMEM(pack, BF16),
            pltpu.VMEM(pack, BF16),
            pltpu.VMEM((blocks, BLOCK, 2 * rank), BF16),
            dma((3,)),
            dma,
            dma((2,)),
            dma((moving,)),
            dma((moving,)),
            dma((moving,)),
            dma((moving,)),
            dma,
            dma((2 * n_sp,)),
            dma((2 * n_sp,)),
            dma,
            dma((2 * n_sp,)),
            dma((2 * n_sp,)),
            dma((2,)),
            dma((2,)),
            dma((per,)),
            dma((per,)),
        ],
        compiler_params=pltpu.CompilerParams(
            collective_id=0,
            has_side_effects=True,
            vmem_limit_bytes=48 * 1024 * 1024,
        ),
    )(
        tenant_of_block,
        token_rows_per_block,
        tenant_table_row,
        activations,
        output_projection_weight,
        turned,
        expand_matrices,
    )


def solution(mesh):
    in_specs = (
        P(("groups", "sp"), "tp"),
        P("tp", None),
        P(("sp", "ep"), "tp", None),
        P(("sp", "ep"), None, "tp"),
        P(("groups", "sp")),
        P(("groups", "sp")),
        P(),
    )
    return jax.shard_map(
        functools.partial(
            per_device, mesh.shape["tp"], mesh.shape["sp"], mesh.shape["ep"]
        ),
        mesh=mesh,
        in_specs=in_specs,
        out_specs=P(("groups", "sp"), "tp"),
        check_vma=False,
    )
```

```python
import functools

import jax
import jax.numpy as jnp
from jax import lax
from jax.experimental import pallas as pl
from jax.experimental.pallas import tpu as pltpu
from jax.sharding import PartitionSpec as P

BLOCK = 128
CHUNK = 512
ENDS = 4
MESH = pl.DeviceIdType.MESH
F32 = jnp.float32
BF16 = jnp.bfloat16


def kernel(
    n,
    n_sp,
    n_ep,
    chunk,
    tenant_hbm,
    live_hbm,
    table_hbm,
    x_hbm,
    w_hbm,
    a_hbm,
    b_hbm,
    o_ref,
    tenant_ref,
    live_ref,
    table_ref,
    x_v,
    w_v,
    prod,
    right,
    left,
    own,
    a_all,
    b_all,
    packs,
    from_left,
    from_right,
    pack_right,
    pack_left,
    lhs,
    int_sem,
    x_sem,
    w_sem,
    right_send,
    right_recv,
    left_send,
    left_recv,
    end_right_send,
    end_right_recv,
    end_left_send,
    end_left_recv,
    a_local,
    a_send,
    a_recv,
    b_local,
    b_send,
    b_recv,
    pack_send,
    pack_recv,
    out_send,
    out_recv,
):
    z = lax.axis_index("tp")
    s = lax.axis_index("sp")
    e = lax.axis_index("ep")
    rows = x_v.shape[0]
    width = o_ref.shape[1]
    per = width // chunk
    blocks = rows // BLOCK
    pieces = a_hbm.shape[0]
    moving = (n - 1) * per
    row0 = pl.multiple_of(e * rows, BLOCK)

    half = rows // 2
    halves = [pl.ds(h * half, half) for h in range(2)]
    x_copies = [
        pltpu.make_async_copy(
            x_hbm.at[pl.ds(row0 + h * half, half), :], x_v.at[halves[h]], x_sem.at[h]
        )
        for h in range(2)
    ]

    n_right = (n - 1 - z) * per
    n_left = z * per
    in_low = z < n // 2
    n_first = jnp.where(in_low, n_right, n_left)
    n_second = moving - n_first

    def item(i):
        paired = i <= 2 * n_second
        odd = i % 2
        index = jnp.where(
            paired,
            jnp.where(odd == 1, (i + 1) // 2, jnp.where(i == 0, 0, i // 2 - 1)),
            i - n_second,
        )
        second = jnp.where(paired & (odd == 0) & (i > 0), 1, 0)
        is_own = i >= moving
        goes_right = jnp.where(in_low, 1 - second, second)
        kind = jnp.where(is_own, 2, jnp.where(goes_right == 1, 0, 1))
        index = jnp.where(is_own, i - moving, index)
        return kind, index

    def column_of(i):
        kind, index = item(i)
        steps = index // per
        dest = jnp.where(kind == 2, z, jnp.where(kind == 0, n - 1 - steps, steps))
        return pl.multiple_of(dest * width + (index % per) * chunk, chunk)

    def w_copy(i):
        slot = i % 2
        return pltpu.make_async_copy(
            w_hbm.at[:, pl.ds(column_of(i), chunk)], w_v.at[slot], w_sem.at[slot]
        )

    w_copy(0).start()
    for copy in x_copies:
        copy.start()

    int_copies = [
        pltpu.make_async_copy(src, dst, int_sem.at[k])
        for k, (src, dst) in enumerate(
            ((tenant_hbm, tenant_ref), (live_hbm, live_ref), (table_hbm, table_ref))
        )
    ]

    barrier = pltpu.get_barrier_semaphore()

    def greet(device_id):
        pl.semaphore_signal(barrier, inc=1, device_id=device_id, device_id_type=MESH)

    @pl.when(z > 0)
    def _():
        greet({"tp": z - 1})

    @pl.when(z < n - 1)
    def _():
        greet({"tp": z + 1})

    for k in range(1, n_sp):
        greet({"sp": lax.rem(s + k, n_sp)})
    for k in range(1, n_ep):
        greet({"ep": lax.rem(e + k, n_ep)})
    line_ends = jnp.where(z > 0, 1, 0) + jnp.where(z < n - 1, 1, 0)
    greeters = line_ends + (n_sp - 1) + (n_ep - 1)

    sibling = {"ep": lax.rem(e + 1, n_ep)}

    def part(ref, owner_s, owner_e):
        start = (owner_s * n_ep + owner_e) * pieces
        return ref.at[pl.ds(start, pieces)]

    def along_sp(src, gathered, send, recv, k):
        return pltpu.make_async_remote_copy(
            src_ref=src,
            dst_ref=part(gathered, s, e),
            send_sem=send.at[k],
            recv_sem=recv.at[k],
            device_id={"sp": lax.rem(s + k, n_sp)},
            device_id_type=MESH,
        )

    def along_ep(src, gathered, send, recv, k):
        return pltpu.make_async_remote_copy(
            src_ref=src,
            dst_ref=part(gathered, lax.rem(s + n_sp - k, n_sp), e),
            send_sem=send.at[n_sp + k],
            recv_sem=recv.at[n_sp + k],
            device_id=sibling,
            device_id_type=MESH,
        )

    tables = (
        (a_hbm, a_all, a_local, a_send, a_recv),
        (b_hbm, b_all, b_local, b_send, b_recv),
    )

    def start_table(src, gathered, local, send, recv):
        for k in range(1, n_sp):
            along_sp(src, gathered, send, recv, k).start()
        along_ep(src, gathered, send, recv, 0).start()
        pltpu.make_async_copy(src, part(gathered, s, e), local).start()

    def forward_table(src, gathered, local, send, recv):
        for k in range(1, n_sp):
            along_sp(src, gathered, send, recv, k).wait_recv()
            piece = part(gathered, lax.rem(s + n_sp - k, n_sp), e)
            along_ep(piece, gathered, send, recv, k).start()

    def finish_table(src, gathered, local, send, recv):
        pltpu.make_async_copy(src, part(gathered, s, e), local).wait()
        for k in range(n_sp):
            along_ep(src, gathered, send, recv, k).wait_recv()

    def drain_table(src, gathered, local, send, recv):
        for k in range(1, n_sp):
            along_sp(src, gathered, send, recv, k).wait_send()
        for k in range(n_sp):
            along_ep(src, gathered, send, recv, k).wait_send()

    def along_line(ref, t, send, recv, to, place=None):
        piece = ref.at[t] if place is None else ref.at[t, place]
        return pltpu.make_async_remote_copy(
            src_ref=piece,
            dst_ref=piece,
            send_sem=send,
            recv_sem=recv,
            device_id={"tp": to},
            device_id_type=MESH,
        )

    def right_copy(t, place=None):
        return along_line(right, t, right_send.at[t], right_recv.at[t], z + 1, place)

    def left_copy(t, place=None):
        return along_line(left, t, left_send.at[t], left_recv.at[t], z - 1, place)

    fine = rows // ENDS
    parts = [pl.ds(q * fine, fine) for q in range(ENDS)]

    def right_end(t, q):
        return along_line(
            right, t, end_right_send.at[q], end_right_recv.at[q], z + 1, parts[q]
        )

    def left_end(t, q):
        return along_line(
            left, t, end_left_send.at[q], end_left_recv.at[q], z - 1, parts[q]
        )

    def pack_right_copy():
        return pltpu.make_async_remote_copy(
            src_ref=pack_right,
            dst_ref=pack_right,
            send_sem=pack_send.at[0],
            recv_sem=pack_recv.at[0],
            device_id={"tp": z + 1},
            device_id_type=MESH,
        )

    def pack_left_copy():
        return pltpu.make_async_remote_copy(
            src_ref=pack_left,
            dst_ref=pack_left,
            send_sem=pack_send.at[1],
            recv_sem=pack_recv.at[1],
            device_id={"tp": z - 1},
            device_id_type=MESH,
        )

    def multiply(i):
        slot = i % 2

        @pl.when(i + 1 < n * per)
        def _():
            w_copy(i + 1).start()

        w_copy(i).wait()
        prod[...] = jnp.dot(x_v[...], w_v[slot], preferred_element_type=F32)

    def pass_on(i):
        kind, t = item(i)

        @pl.when(kind == 0)
        def _():
            @pl.when(z > 0)
            def _():
                right_copy(t).wait_recv()
                right[t] = (prod[...] + right[t].astype(F32)).astype(BF16)

            @pl.when(z == 0)
            def _():
                right[t] = prod[...].astype(BF16)

            @pl.when(t < n_right - 1)
            def _():
                right_copy(t).start()

            @pl.when(t == n_right - 1)
            def _():
                for q in range(ENDS):
                    right_end(t, q).start()

        @pl.when(kind == 1)
        def _():
            @pl.when(z < n - 1)
            def _():
                left_copy(t).wait_recv()
                left[t] = (prod[...] + left[t].astype(F32)).astype(BF16)

            @pl.when(z == n - 1)
            def _():
                left[t] = prod[...].astype(BF16)

            @pl.when(t < n_left - 1)
            def _():
                left_copy(t).start()

            @pl.when(t == n_left - 1)
            def _():
                for q in range(ENDS):
                    left_end(t, q).start()

        @pl.when(kind == 2)
        def _():
            own[t] = prod[...]

    def step(i, carry):
        multiply(i)
        pass_on(i)
        return carry

    w_copy(1).start()
    w_copy(0).wait()
    for h in range(2):
        x_copies[h].wait()
        prod[halves[h], :] = jnp.dot(
            x_v[halves[h], :], w_v[0], preferred_element_type=F32
        )
        if h == 0:
            pl.semaphore_wait(barrier, greeters)

        @pl.when(z == 0)
        def _():
            right[0, halves[h], :] = prod[halves[h], :].astype(BF16)
            right_copy(0, halves[h]).start()

        @pl.when(z == n - 1)
        def _():
            left[0, halves[h], :] = prod[halves[h], :].astype(BF16)
            left_copy(0, halves[h]).start()

    @pl.when((z > 0) & (z < n - 1))
    def _():
        pass_on(0)

    start_table(*tables[0])
    start_table(*tables[1])
    for copy in int_copies:
        copy.start()
    turn_a = max(1, moving * 5 // 12)
    turn_b = max(1, moving * 7 // 12)
    lax.fori_loop(1, turn_a, step, 0)
    forward_table(*tables[0])
    lax.fori_loop(turn_a, turn_b, step, 0)
    finish_table(*tables[0])
    for copy in int_copies:
        copy.wait()

    rank = b_hbm.shape[1]
    lane = lax.broadcasted_iota(jnp.int32, (BLOCK, 2 * rank), 1)

    def shrink_twice(b):
        slot = table_ref[tenant_ref[e * blocks + b]]
        matrix = a_all[slot]
        return lax.dot_general(
            x_v[b * BLOCK : (b + 1) * BLOCK, :],
            jnp.concatenate([matrix, matrix], axis=0),
            (((1,), (1,)), ((), ())),
            preferred_element_type=F32,
        )

    for p in range(blocks // 2):
        packs[p] = jnp.where(
            lane < rank, shrink_twice(2 * p), shrink_twice(2 * p + 1)
        )

    @pl.when(z == 0)
    def _():
        pack_right[...] = packs[...].astype(BF16)
        pack_right_copy().start()

    @pl.when(z == n - 1)
    def _():
        pack_left[...] = packs[...].astype(BF16)
        pack_left_copy().start()

    lax.fori_loop(turn_b, moving, step, 0)

    def pass_right():
        @pl.when(z > 0)
        def _():
            pack_right_copy().wait_recv()
            from_left[...] = pack_right[...].astype(F32)

            @pl.when(z < n - 1)
            def _():
                pack_right[...] = (packs[...] + from_left[...]).astype(BF16)
                pack_right_copy().start()

    def pass_left():
        @pl.when(z < n - 1)
        def _():
            pack_left_copy().wait_recv()
            from_right[...] = pack_left[...].astype(F32)

            @pl.when(z > 0)
            def _():
                pack_left[...] = (packs[...] + from_right[...]).astype(BF16)
                pack_left_copy().start()

    from_left[...] = jnp.zeros_like(from_left)
    from_right[...] = jnp.zeros_like(from_right)

    @pl.when(in_low)
    def _():
        pass_right()

    pass_left()

    @pl.when(jnp.logical_not(in_low))
    def _():
        pass_right()

    lax.fori_loop(moving, n * per, step, 0)
    forward_table(*tables[1])

    row = lax.broadcasted_iota(jnp.int32, (BLOCK, 2 * rank), 0)
    for p in range(blocks // 2):
        total = packs[p] + from_left[p] + from_right[p]
        for side in range(2):
            b = 2 * p + side
            mine = (lane < rank) if side == 0 else (lane >= rank)
            keep = mine & (row < live_ref[e * blocks + b])
            lhs[b] = jnp.where(keep, total, 0.0).astype(BF16)

    finish_table(*tables[1])
    for b in range(blocks):
        slot = table_ref[tenant_ref[e * blocks + b]]
        matrix = b_all[slot]
        stacked = jnp.concatenate([matrix, matrix], axis=0)
        for j in range(per):
            own[j, b * BLOCK : (b + 1) * BLOCK, :] += jnp.dot(
                lhs[b],
                stacked[:, j * chunk : (j + 1) * chunk],
                preferred_element_type=F32,
            )

    whole = [pl.ds(0, rows)]

    def spans(j):
        return parts if j == per - 1 else whole

    def out_remote(j, q):
        span = spans(j)[q]
        place = o_ref.at[
            pl.ds(pl.multiple_of(row0 + span.start, span.size), span.size),
            pl.ds(j * chunk, chunk),
        ]
        return pltpu.make_async_remote_copy(
            src_ref=place,
            dst_ref=place,
            send_sem=out_send.at[j + q],
            recv_sem=out_recv.at[j + q],
            device_id=sibling,
            device_id_type=MESH,
        )

    def take_left(j, q):
        t = z * per + j
        (left_end(t, q) if j == per - 1 else left_copy(t)).wait_recv()
        return left[t, spans(j)[q], :].astype(F32)

    def take_right(j, q):
        t = (n - 1 - z) * per + j
        (right_end(t, q) if j == per - 1 else right_copy(t)).wait_recv()
        return right[t, spans(j)[q], :].astype(F32)

    def finish(j, q, value):
        span = spans(j)[q]
        start = pl.multiple_of(row0 + span.start, span.size)
        o_ref[pl.ds(start, span.size), j * chunk : (j + 1) * chunk] = value.astype(BF16)
        out_remote(j, q).start()

    pieces_out = [(j, q) for j in range(per) for q in range(len(spans(j)))]

    @pl.when(in_low)
    def _():
        for j, q in pieces_out:
            own[j, spans(j)[q], :] += take_left(j, q)

        @pl.when(z > 0)
        def _():
            for j, q in pieces_out:
                finish(j, q, own[j, spans(j)[q], :] + take_right(j, q))

    @pl.when(jnp.logical_not(in_low))
    def _():
        for j, q in pieces_out:
            own[j, spans(j)[q], :] += take_right(j, q)

        @pl.when(z < n - 1)
        def _():
            for j, q in pieces_out:
                finish(j, q, own[j, spans(j)[q], :] + take_left(j, q))

    @pl.when((z == 0) | (z == n - 1))
    def _():
        for j, q in pieces_out:
            finish(j, q, own[j, spans(j)[q], :])

    def right_done(t, carry):
        right_copy(t).wait_send()
        return carry

    def left_done(t, carry):
        left_copy(t).wait_send()
        return carry

    lax.fori_loop(0, n_right - 1, right_done, 0)
    lax.fori_loop(0, n_left - 1, left_done, 0)
    drain_table(*tables[0])
    drain_table(*tables[1])

    @pl.when(z < n - 1)
    def _():
        for q in range(ENDS):
            right_end(n_right - 1, q).wait_send()
        pack_right_copy().wait_send()

    @pl.when(z > 0)
    def _():
        for q in range(ENDS):
            left_end(n_left - 1, q).wait_send()
        pack_left_copy().wait_send()

    for j, q in pieces_out:
        out_remote(j, q).wait()


def per_device(
    n,
    n_sp,
    n_ep,
    activations,
    output_projection_weight,
    shrink_matrices,
    expand_matrices,
    tenant_of_block,
    token_rows_per_block,
    tenant_table_row,
):
    all_rows, depth = activations.shape
    rows = all_rows // n_ep
    width = expand_matrices.shape[2]
    chunk = min(CHUNK, width)
    per = width // chunk
    blocks = rows // BLOCK
    pieces, _, rank = shrink_matrices.shape
    count = pieces * n_sp * n_ep
    turned = jnp.swapaxes(shrink_matrices, 1, 2)
    pack = (blocks // 2, BLOCK, 2 * rank)
    moving = (n - 1) * per
    dma = pltpu.SemaphoreType.DMA
    in_hbm = pl.BlockSpec(memory_space=pltpu.HBM)
    return pl.pallas_call(
        functools.partial(kernel, n, n_sp, n_ep, chunk),
        out_shape=pltpu.VMEM((all_rows, width), BF16),
        in_specs=[in_hbm] * 7,
        out_specs=pl.BlockSpec(memory_space=pltpu.VMEM),
        scratch_shapes=[
            pltpu.SMEM(tenant_of_block.shape, jnp.int32),
            pltpu.SMEM(token_rows_per_block.shape, jnp.int32),
            pltpu.SMEM(tenant_table_row.shape, jnp.int32),
            pltpu.VMEM((rows, depth), BF16),
            pltpu.VMEM((2, depth, chunk), BF16),
            pltpu.VMEM((rows, chunk), F32),
            pltpu.VMEM((moving, rows, chunk), BF16),
            pltpu.VMEM((moving, rows, chunk), BF16),
            pltpu.VMEM((per, rows, chunk), F32),
            pltpu.VMEM((count, rank, depth), BF16),
            pltpu.VMEM((count, rank, width), BF16),
            pltpu.VMEM(pack, F32),
            pltpu.VMEM(pack, F32),
            pltpu.VMEM(pack, F32),
            pltpu.VMEM(pack, BF16),
            pltpu.VMEM(pack, BF16),
            pltpu.VMEM((blocks, BLOCK, 2 * rank), BF16),
            dma((3,)),
            dma((2,)),
            dma((2,)),
            dma((moving,)),
            dma((moving,)),
            dma((moving,)),
            dma((moving,)),
            dma((ENDS,)),
            dma((ENDS,)),
            dma((ENDS,)),
            dma((ENDS,)),
            dma,
            dma((2 * n_sp,)),
            dma((2 * n_sp,)),
            dma,
            dma((2 * n_sp,)),
            dma((2 * n_sp,)),
            dma((2,)),
            dma((2,)),
            dma((per - 1 + ENDS,)),
            dma((per - 1 + ENDS,)),
        ],
        compiler_params=pltpu.CompilerParams(
            collective_id=0,
            has_side_effects=True,
            vmem_limit_bytes=48 * 1024 * 1024,
        ),
    )(
        pltpu.with_memory_space_constraint(tenant_of_block, pltpu.HBM),
        pltpu.with_memory_space_constraint(token_rows_per_block, pltpu.HBM),
        pltpu.with_memory_space_constraint(tenant_table_row, pltpu.HBM),
        activations,
        output_projection_weight,
        turned,
        expand_matrices,
    )


def solution(mesh):
    in_specs = (
        P(("groups", "sp"), "tp"),
        P("tp", None),
        P(("sp", "ep"), "tp", None),
        P(("sp", "ep"), None, "tp"),
        P(("groups", "sp")),
        P(("groups", "sp")),
        P(),
    )
    return jax.shard_map(
        functools.partial(
            per_device, mesh.shape["tp"], mesh.shape["sp"], mesh.shape["ep"]
        ),
        mesh=mesh,
        in_specs=in_specs,
        out_specs=P(("groups", "sp"), "tp"),
        check_vma=False,
    )
```

```python
import functools

import jax
import jax.numpy as jnp
from jax import lax
from jax.experimental import pallas as pl
from jax.experimental.pallas import tpu as pltpu
from jax.sharding import PartitionSpec as P

BLOCK = 128
CHUNK = 512
ENDS = 8
MESH = pl.DeviceIdType.MESH
F32 = jnp.float32
BF16 = jnp.bfloat16


def kernel(
    n,
    n_sp,
    n_ep,
    chunk,
    tenant_hbm,
    live_hbm,
    table_hbm,
    x_hbm,
    w_hbm,
    a_hbm,
    b_hbm,
    o_ref,
    tenant_ref,
    live_ref,
    table_ref,
    x_v,
    w_v,
    prod,
    right,
    left,
    own,
    a_all,
    b_all,
    packs,
    from_left,
    from_right,
    pack_right,
    pack_left,
    lhs,
    int_sem,
    x_sem,
    w_sem,
    right_send,
    right_recv,
    left_send,
    left_recv,
    end_right_send,
    end_right_recv,
    end_left_send,
    end_left_recv,
    a_local,
    a_send,
    a_recv,
    b_local,
    b_send,
    b_recv,
    pack_send,
    pack_recv,
    out_send,
    out_recv,
):
    z = lax.axis_index("tp")
    s = lax.axis_index("sp")
    e = lax.axis_index("ep")
    rows = x_v.shape[0]
    width = o_ref.shape[1]
    per = width // chunk
    blocks = rows // BLOCK
    pieces = a_hbm.shape[0]
    moving = (n - 1) * per
    row0 = pl.multiple_of(e * rows, BLOCK)

    half = rows // 2
    halves = [pl.ds(h * half, half) for h in range(2)]
    x_copies = [
        pltpu.make_async_copy(
            x_hbm.at[pl.ds(row0 + h * half, half), :], x_v.at[halves[h]], x_sem.at[h]
        )
        for h in range(2)
    ]

    n_right = (n - 1 - z) * per
    n_left = z * per
    in_low = z < n // 2
    n_first = jnp.where(in_low, n_right, n_left)
    n_second = moving - n_first

    def item(i):
        paired = i <= 2 * n_second
        odd = i % 2
        index = jnp.where(
            paired,
            jnp.where(odd == 1, (i + 1) // 2, jnp.where(i == 0, 0, i // 2 - 1)),
            i - n_second,
        )
        second = jnp.where(paired & (odd == 0) & (i > 0), 1, 0)
        is_own = i >= moving
        goes_right = jnp.where(in_low, 1 - second, second)
        kind = jnp.where(is_own, 2, jnp.where(goes_right == 1, 0, 1))
        index = jnp.where(is_own, i - moving, index)
        return kind, index

    def column_of(i):
        kind, index = item(i)
        steps = index // per
        dest = jnp.where(kind == 2, z, jnp.where(kind == 0, n - 1 - steps, steps))
        return pl.multiple_of(dest * width + (index % per) * chunk, chunk)

    def w_copy(i):
        slot = i % 2
        return pltpu.make_async_copy(
            w_hbm.at[:, pl.ds(column_of(i), chunk)], w_v.at[slot], w_sem.at[slot]
        )

    w_copy(0).start()
    for copy in x_copies:
        copy.start()

    int_copies = [
        pltpu.make_async_copy(src, dst, int_sem.at[k])
        for k, (src, dst) in enumerate(
            ((tenant_hbm, tenant_ref), (live_hbm, live_ref), (table_hbm, table_ref))
        )
    ]

    barrier = pltpu.get_barrier_semaphore()

    def greet(device_id):
        pl.semaphore_signal(barrier, inc=1, device_id=device_id, device_id_type=MESH)

    @pl.when(z > 0)
    def _():
        greet({"tp": z - 1})

    @pl.when(z < n - 1)
    def _():
        greet({"tp": z + 1})

    for k in range(1, n_sp):
        greet({"sp": lax.rem(s + k, n_sp)})
    for k in range(1, n_ep):
        greet({"ep": lax.rem(e + k, n_ep)})
    line_ends = jnp.where(z > 0, 1, 0) + jnp.where(z < n - 1, 1, 0)
    greeters = line_ends + (n_sp - 1) + (n_ep - 1)

    sibling = {"ep": lax.rem(e + 1, n_ep)}

    def part(ref, owner_s, owner_e):
        start = (owner_s * n_ep + owner_e) * pieces
        return ref.at[pl.ds(start, pieces)]

    def along_sp(src, gathered, send, recv, k):
        return pltpu.make_async_remote_copy(
            src_ref=src,
            dst_ref=part(gathered, s, e),
            send_sem=send.at[k],
            recv_sem=recv.at[k],
            device_id={"sp": lax.rem(s + k, n_sp)},
            device_id_type=MESH,
        )

    def along_ep(src, gathered, send, recv, k):
        return pltpu.make_async_remote_copy(
            src_ref=src,
            dst_ref=part(gathered, lax.rem(s + n_sp - k, n_sp), e),
            send_sem=send.at[n_sp + k],
            recv_sem=recv.at[n_sp + k],
            device_id=sibling,
            device_id_type=MESH,
        )

    tables = (
        (a_hbm, a_all, a_local, a_send, a_recv),
        (b_hbm, b_all, b_local, b_send, b_recv),
    )

    def start_table(src, gathered, local, send, recv):
        for k in range(1, n_sp):
            along_sp(src, gathered, send, recv, k).start()
        along_ep(src, gathered, send, recv, 0).start()
        pltpu.make_async_copy(src, part(gathered, s, e), local).start()

    def forward_table(src, gathered, local, send, recv):
        for k in range(1, n_sp):
            along_sp(src, gathered, send, recv, k).wait_recv()
            piece = part(gathered, lax.rem(s + n_sp - k, n_sp), e)
            along_ep(piece, gathered, send, recv, k).start()

    def finish_table(src, gathered, local, send, recv):
        pltpu.make_async_copy(src, part(gathered, s, e), local).wait()
        for k in range(n_sp):
            along_ep(src, gathered, send, recv, k).wait_recv()

    def drain_table(src, gathered, local, send, recv):
        for k in range(1, n_sp):
            along_sp(src, gathered, send, recv, k).wait_send()
        for k in range(n_sp):
            along_ep(src, gathered, send, recv, k).wait_send()

    def along_line(ref, t, send, recv, to, place=None):
        piece = ref.at[t] if place is None else ref.at[t, place]
        return pltpu.make_async_remote_copy(
            src_ref=piece,
            dst_ref=piece,
            send_sem=send,
            recv_sem=recv,
            device_id={"tp": to},
            device_id_type=MESH,
        )

    def right_copy(t, place=None):
        return along_line(right, t, right_send.at[t], right_recv.at[t], z + 1, place)

    def left_copy(t, place=None):
        return along_line(left, t, left_send.at[t], left_recv.at[t], z - 1, place)

    fine = rows // ENDS
    parts = [pl.ds(q * fine, fine) for q in range(ENDS)]

    def right_end(t, q):
        return along_line(
            right, t, end_right_send.at[q], end_right_recv.at[q], z + 1, parts[q]
        )

    def left_end(t, q):
        return along_line(
            left, t, end_left_send.at[q], end_left_recv.at[q], z - 1, parts[q]
        )

    def pack_right_copy():
        return pltpu.make_async_remote_copy(
            src_ref=pack_right,
            dst_ref=pack_right,
            send_sem=pack_send.at[0],
            recv_sem=pack_recv.at[0],
            device_id={"tp": z + 1},
            device_id_type=MESH,
        )

    def pack_left_copy():
        return pltpu.make_async_remote_copy(
            src_ref=pack_left,
            dst_ref=pack_left,
            send_sem=pack_send.at[1],
            recv_sem=pack_recv.at[1],
            device_id={"tp": z - 1},
            device_id_type=MESH,
        )

    def multiply(i):
        slot = i % 2

        @pl.when(i + 1 < n * per)
        def _():
            w_copy(i + 1).start()

        w_copy(i).wait()
        prod[...] = jnp.dot(x_v[...], w_v[slot], preferred_element_type=F32)

    def pass_on(i):
        kind, t = item(i)

        @pl.when(kind == 0)
        def _():
            @pl.when(z > 0)
            def _():
                right_copy(t).wait_recv()
                right[t] = (prod[...] + right[t].astype(F32)).astype(BF16)

            @pl.when(z == 0)
            def _():
                right[t] = prod[...].astype(BF16)

            @pl.when(t < n_right - 1)
            def _():
                right_copy(t).start()

            @pl.when(t == n_right - 1)
            def _():
                for q in range(ENDS):
                    right_end(t, q).start()

        @pl.when(kind == 1)
        def _():
            @pl.when(z < n - 1)
            def _():
                left_copy(t).wait_recv()
                left[t] = (prod[...] + left[t].astype(F32)).astype(BF16)

            @pl.when(z == n - 1)
            def _():
                left[t] = prod[...].astype(BF16)

            @pl.when(t < n_left - 1)
            def _():
                left_copy(t).start()

            @pl.when(t == n_left - 1)
            def _():
                for q in range(ENDS):
                    left_end(t, q).start()

        @pl.when(kind == 2)
        def _():
            own[t] = prod[...]

    def step(i, carry):
        multiply(i)
        pass_on(i)
        return carry

    w_copy(1).start()
    w_copy(0).wait()
    for h in range(2):
        x_copies[h].wait()
        prod[halves[h], :] = jnp.dot(
            x_v[halves[h], :], w_v[0], preferred_element_type=F32
        )
        if h == 0:
            pl.semaphore_wait(barrier, greeters)

        @pl.when(z == 0)
        def _():
            right[0, halves[h], :] = prod[halves[h], :].astype(BF16)
            right_copy(0, halves[h]).start()

        @pl.when(z == n - 1)
        def _():
            left[0, halves[h], :] = prod[halves[h], :].astype(BF16)
            left_copy(0, halves[h]).start()

    @pl.when((z > 0) & (z < n - 1))
    def _():
        pass_on(0)

    start_table(*tables[0])
    start_table(*tables[1])
    for copy in int_copies:
        copy.start()
    turn_a = max(1, moving * 5 // 12)
    turn_b = max(1, moving * 7 // 12)
    lax.fori_loop(1, turn_a, step, 0)
    forward_table(*tables[0])
    lax.fori_loop(turn_a, turn_b, step, 0)
    finish_table(*tables[0])
    for copy in int_copies:
        copy.wait()

    rank = b_hbm.shape[1]
    lane = lax.broadcasted_iota(jnp.int32, (BLOCK, 2 * rank), 1)

    def shrink_twice(b):
        slot = table_ref[tenant_ref[e * blocks + b]]
        matrix = a_all[slot]
        return lax.dot_general(
            x_v[b * BLOCK : (b + 1) * BLOCK, :],
            jnp.concatenate([matrix, matrix], axis=0),
            (((1,), (1,)), ((), ())),
            preferred_element_type=F32,
        )

    for p in range(blocks // 2):
        packs[p] = jnp.where(
            lane < rank, shrink_twice(2 * p), shrink_twice(2 * p + 1)
        )

    @pl.when(z == 0)
    def _():
        pack_right[...] = packs[...].astype(BF16)
        pack_right_copy().start()

    @pl.when(z == n - 1)
    def _():
        pack_left[...] = packs[...].astype(BF16)
        pack_left_copy().start()

    lax.fori_loop(turn_b, moving, step, 0)

    def pass_right():
        @pl.when(z > 0)
        def _():
            pack_right_copy().wait_recv()
            from_left[...] = pack_right[...].astype(F32)

            @pl.when(z < n - 1)
            def _():
                pack_right[...] = (packs[...] + from_left[...]).astype(BF16)
                pack_right_copy().start()

    def pass_left():
        @pl.when(z < n - 1)
        def _():
            pack_left_copy().wait_recv()
            from_right[...] = pack_left[...].astype(F32)

            @pl.when(z > 0)
            def _():
                pack_left[...] = (packs[...] + from_right[...]).astype(BF16)
                pack_left_copy().start()

    from_left[...] = jnp.zeros_like(from_left)
    from_right[...] = jnp.zeros_like(from_right)

    @pl.when(in_low)
    def _():
        pass_right()

    pass_left()

    @pl.when(jnp.logical_not(in_low))
    def _():
        pass_right()

    lax.fori_loop(moving, n * per, step, 0)
    forward_table(*tables[1])

    row = lax.broadcasted_iota(jnp.int32, (BLOCK, 2 * rank), 0)
    for p in range(blocks // 2):
        total = packs[p] + from_left[p] + from_right[p]
        for side in range(2):
            b = 2 * p + side
            mine = (lane < rank) if side == 0 else (lane >= rank)
            keep = mine & (row < live_ref[e * blocks + b])
            lhs[b] = jnp.where(keep, total, 0.0).astype(BF16)

    finish_table(*tables[1])
    for b in range(blocks):
        slot = table_ref[tenant_ref[e * blocks + b]]
        matrix = b_all[slot]
        stacked = jnp.concatenate([matrix, matrix], axis=0)
        for j in range(per):
            own[j, b * BLOCK : (b + 1) * BLOCK, :] += jnp.dot(
                lhs[b],
                stacked[:, j * chunk : (j + 1) * chunk],
                preferred_element_type=F32,
            )

    whole = [pl.ds(0, rows)]

    def spans(j):
        return parts if j == per - 1 else whole

    def out_remote(j, q):
        span = spans(j)[q]
        place = o_ref.at[
            pl.ds(pl.multiple_of(row0 + span.start, span.size), span.size),
            pl.ds(j * chunk, chunk),
        ]
        return pltpu.make_async_remote_copy(
            src_ref=place,
            dst_ref=place,
            send_sem=out_send.at[j + q],
            recv_sem=out_recv.at[j + q],
            device_id=sibling,
            device_id_type=MESH,
        )

    def take_left(j, q):
        t = z * per + j
        (left_end(t, q) if j == per - 1 else left_copy(t)).wait_recv()
        return left[t, spans(j)[q], :].astype(F32)

    def take_right(j, q):
        t = (n - 1 - z) * per + j
        (right_end(t, q) if j == per - 1 else right_copy(t)).wait_recv()
        return right[t, spans(j)[q], :].astype(F32)

    def finish(j, q, value):
        span = spans(j)[q]
        start = pl.multiple_of(row0 + span.start, span.size)
        o_ref[pl.ds(start, span.size), j * chunk : (j + 1) * chunk] = value.astype(BF16)
        out_remote(j, q).start()

    pieces_out = [(j, q) for j in range(per) for q in range(len(spans(j)))]

    @pl.when(in_low)
    def _():
        for j, q in pieces_out:
            own[j, spans(j)[q], :] += take_left(j, q)

        @pl.when(z > 0)
        def _():
            for j, q in pieces_out:
                finish(j, q, own[j, spans(j)[q], :] + take_right(j, q))

    @pl.when(jnp.logical_not(in_low))
    def _():
        for j, q in pieces_out:
            own[j, spans(j)[q], :] += take_right(j, q)

        @pl.when(z < n - 1)
        def _():
            for j, q in pieces_out:
                finish(j, q, own[j, spans(j)[q], :] + take_left(j, q))

    @pl.when((z == 0) | (z == n - 1))
    def _():
        for j, q in pieces_out:
            finish(j, q, own[j, spans(j)[q], :])

    def right_done(t, carry):
        right_copy(t).wait_send()
        return carry

    def left_done(t, carry):
        left_copy(t).wait_send()
        return carry

    lax.fori_loop(0, n_right - 1, right_done, 0)
    lax.fori_loop(0, n_left - 1, left_done, 0)
    drain_table(*tables[0])
    drain_table(*tables[1])

    @pl.when(z < n - 1)
    def _():
        for q in range(ENDS):
            right_end(n_right - 1, q).wait_send()
        pack_right_copy().wait_send()

    @pl.when(z > 0)
    def _():
        for q in range(ENDS):
            left_end(n_left - 1, q).wait_send()
        pack_left_copy().wait_send()

    for j, q in pieces_out:
        out_remote(j, q).wait()


def per_device(
    n,
    n_sp,
    n_ep,
    activations,
    output_projection_weight,
    shrink_matrices,
    expand_matrices,
    tenant_of_block,
    token_rows_per_block,
    tenant_table_row,
):
    all_rows, depth = activations.shape
    rows = all_rows // n_ep
    width = expand_matrices.shape[2]
    chunk = min(CHUNK, width)
    per = width // chunk
    blocks = rows // BLOCK
    pieces, _, rank = shrink_matrices.shape
    count = pieces * n_sp * n_ep
    turned = jnp.swapaxes(shrink_matrices, 1, 2)
    pack = (blocks // 2, BLOCK, 2 * rank)
    moving = (n - 1) * per
    dma = pltpu.SemaphoreType.DMA
    in_hbm = pl.BlockSpec(memory_space=pltpu.HBM)
    return pl.pallas_call(
        functools.partial(kernel, n, n_sp, n_ep, chunk),
        out_shape=pltpu.VMEM((all_rows, width), BF16),
        in_specs=[in_hbm] * 7,
        out_specs=pl.BlockSpec(memory_space=pltpu.VMEM),
        scratch_shapes=[
            pltpu.SMEM(tenant_of_block.shape, jnp.int32),
            pltpu.SMEM(token_rows_per_block.shape, jnp.int32),
            pltpu.SMEM(tenant_table_row.shape, jnp.int32),
            pltpu.VMEM((rows, depth), BF16),
            pltpu.VMEM((2, depth, chunk), BF16),
            pltpu.VMEM((rows, chunk), F32),
            pltpu.VMEM((moving, rows, chunk), BF16),
            pltpu.VMEM((moving, rows, chunk), BF16),
            pltpu.VMEM((per, rows, chunk), F32),
            pltpu.VMEM((count, rank, depth), BF16),
            pltpu.VMEM((count, rank, width), BF16),
            pltpu.VMEM(pack, F32),
            pltpu.VMEM(pack, F32),
            pltpu.VMEM(pack, F32),
            pltpu.VMEM(pack, BF16),
            pltpu.VMEM(pack, BF16),
            pltpu.VMEM((blocks, BLOCK, 2 * rank), BF16),
            dma((3,)),
            dma((2,)),
            dma((2,)),
            dma((moving,)),
            dma((moving,)),
            dma((moving,)),
            dma((moving,)),
            dma((ENDS,)),
            dma((ENDS,)),
            dma((ENDS,)),
            dma((ENDS,)),
            dma,
            dma((2 * n_sp,)),
            dma((2 * n_sp,)),
            dma,
            dma((2 * n_sp,)),
            dma((2 * n_sp,)),
            dma((2,)),
            dma((2,)),
            dma((per - 1 + ENDS,)),
            dma((per - 1 + ENDS,)),
        ],
        compiler_params=pltpu.CompilerParams(
            collective_id=0,
            has_side_effects=True,
            vmem_limit_bytes=48 * 1024 * 1024,
        ),
    )(
        pltpu.with_memory_space_constraint(tenant_of_block, pltpu.HBM),
        pltpu.with_memory_space_constraint(token_rows_per_block, pltpu.HBM),
        pltpu.with_memory_space_constraint(tenant_table_row, pltpu.HBM),
        activations,
        output_projection_weight,
        turned,
        expand_matrices,
    )


def solution(mesh):
    in_specs = (
        P(("groups", "sp"), "tp"),
        P("tp", None),
        P(("sp", "ep"), "tp", None),
        P(("sp", "ep"), None, "tp"),
        P(("groups", "sp")),
        P(("groups", "sp")),
        P(),
    )
    return jax.shard_map(
        functools.partial(
            per_device, mesh.shape["tp"], mesh.shape["sp"], mesh.shape["ep"]
        ),
        mesh=mesh,
        in_specs=in_specs,
        out_specs=P(("groups", "sp"), "tp"),
        check_vma=False,
    )
```
